256 devices in a mesh: ep: 128 (over z, y, x), tp: 2 (over core).
Axes of the slice: x: 4, y: 4, z: 8, core: 2. Of those that a mesh axis runs over, the one named last changes fastest.
Arguments:
- tokens: bfloat16 [16384, 4096], P('ep', 'tp'), may hold values from -6 to 6
- expert_ids: int32 [16384, 8], P('ep'), may hold values from 0 to 127, all different within a row; in each aligned block of 128 rows (0 to 127, 128 to 255, ...) at most 12 rows name the same one
- gate_levels: int32 [16384, 8], P('ep'), may hold values from 32 to 255
- gate_weight: bfloat16 [128, 4096, 768], P('ep', None, 'tp'), may hold values from -0.09375 to 0.09375
- up_weight: bfloat16 [128, 4096, 768], P('ep', None, 'tp'), may hold values from -0.09375 to 0.09375
- down_weight: bfloat16 [128, 768, 4096], P('ep', 'tp'), may hold values from -0.21875 to 0.21875
Outputs:
- mixed: bfloat16 [16384, 4096], P('ep', 'tp')
The draws below stay inside these ranges and needn't reach their ends.
Inputs may be any that keep to these rules, and one draw needn't show every extreme that they name: `expert_ids`: each token names 8 different experts. Among the 128 tokens of one aligned block, no expert is named by more than 12 tokens, and in some blocks one expert is named by exactly 12.
All inputs are finite; a program needn't handle non-finite values.
Results may differ from the reference program's by a relative error of at most 0.011.
Values may be sent and summed in bfloat16 or wider, within the bound.
No kernel may reach another device: no remote copies, remote signals or barrier semaphores. Data moves between devices by JAX's collectives and lax.ppermute only.
A program may use at most 128 MiB of HBM per device.

```python
import math
import jax
import jax.numpy as jnp
import numpy as np
from jax import lax

D = 4096
FF = 768
TOPK = 8
TOK_DEV = 128
EXPERTS = 128
TOKENS = 16384
CAP = 12
N_EP = 128
N_TP = 2


def set_ends(entries, rng, low, largest):
    longest = entries.shape.index(max(entries.shape))
    spots = []
    for shift in (0, 1):
        where = [jax.random.randint(jax.random.fold_in(rng, axis), (), 0, length) for axis, length in enumerate(entries.shape)]
        where[longest] = (where[longest] + shift) % entries.shape[longest]
        spots.append(tuple(where))
    return entries.at[spots[0]].set(low).at[spots[1]].set(largest)


def block_scale(own_key, extent, pieces, smallest, high):
    def one(axis_at, blocks):
        heights = jax.random.uniform(jax.random.fold_in(jax.random.fold_in(own_key, 6), axis_at), (blocks,), jnp.float32, smallest / len(pieces), high / len(pieces))
        return jnp.repeat(jnp.exp(heights), extent[axis_at] // blocks).reshape((-1,) + (1,) * (len(extent) - axis_at - 1))

    loudness = one(*pieces[0])
    for cut in pieces[1:]:
        loudness = loudness * one(*cut)
    return loudness


def deal_out(stream_key, own, number, rows, count, top, limit, skew):
    sequence = jax.random.permutation(stream_key, count)
    heavy_load, ordinary = load_shares(count, rows * top, limit, skew, True), load_shares(count, rows * top, limit, skew, False)
    places = jnp.arange(count)

    def named(tallies, offset_by):
        used = int((tallies > 0).sum())
        fixed = max(1, used // 4)
        shifted = fixed + (places - fixed + offset_by * (used - fixed)) % max(1, count - fixed)
        return jnp.zeros((count,), jnp.int32).at[sequence[jnp.where(places < fixed, places, shifted)]].set(jnp.asarray(tallies, jnp.int32))

    tallies = jnp.where(number % 4 == 0, named(heavy_load, number // 4), named(ordinary, number - number // 4 - 1))
    mixed = jax.random.permutation(jax.random.fold_in(own, 3), count)
    source_of, taker = mixed[0:count // 2 * 2:2], mixed[1:count // 2 * 2:2]
    room = jnp.minimum(tallies[source_of] - 1, limit - tallies[taker]) // 2
    room = jnp.where((source_of == sequence[0]) | (taker == sequence[0]) | (tallies[taker] == 0), 0, jnp.maximum(room, 0))
    shifted = jax.random.randint(jax.random.fold_in(own, 4), (count // 2,), 0, 1 << 20) % (room + 1)
    tallies = tallies.at[source_of].add(-shifted).at[taker].add(shifted)
    labels = jnp.searchsorted(jnp.cumsum(tallies), jnp.arange(rows * top), side="right").astype(jnp.int32)
    table = labels.reshape(top, rows).T
    table = table[jax.random.permutation(jax.random.fold_in(own, 1), rows)]
    offset_by = jax.random.randint(jax.random.fold_in(own, 2), (rows, 1), 0, top)
    return jnp.take_along_axis(table, (jnp.arange(top)[None, :] + offset_by) % top, axis=1)


def load_shares(number_of, total, most, lean, full):
    loads = [(1 << 20) // math.isqrt(standing ** lean) + 1 for standing in range(1, number_of + 1)]
    largest = most if full else min(most, max(-(-total // number_of), total * loads[0] // sum(loads)))
    least = 1 if total - largest >= number_of - 1 else 0
    given, spare = [largest] + [least] * (number_of - 1), total - largest - least * (number_of - 1)
    while spare > 0:
        free = [i for i in range(1, number_of) if given[i] < largest] or [i for i in range(1, number_of) if given[i] < most]
        whole, remaining = sum([loads[i] for i in free]), spare
        for i in free:
            addition = min(most - given[i], max(1, remaining * loads[i] // whole), spare)
            given[i] = given[i] + addition
            spare = spare - addition
    return np.array(given)


def normal_values(rng, shape, spread, bound, shards=(), held_as=jnp.bfloat16):
    array = jax.random.normal(rng, shape, jnp.float32) * spread
    if len(shards) > 0:
        array = block_scale(rng, shape, shards, -0.22, 0.18) * array
    return jnp.clip(array, min=-bound, max=bound).astype(held_as)


def setup_inputs(seed: int = 0) -> dict:
    seeds = jax.random.split(jax.random.key(seed), 7)
    tokens = normal_values(seeds[0], (TOKENS, D), 1.0, 6.0, ((0, 128), (1, 2)))
    expert_ids_keys = jax.random.split(jax.random.fold_in(seeds[1], 1), TOKENS // TOK_DEV)
    expert_ids_turns = jax.random.permutation(jax.random.fold_in(seeds[1], 3), TOKENS // TOK_DEV)
    expert_ids = jax.vmap(lambda own, number: deal_out(jax.random.fold_in(seeds[1], 2), own, number, TOK_DEV, EXPERTS, TOPK, CAP, 2))(expert_ids_keys, expert_ids_turns).reshape((TOKENS, TOPK))
    gate_levels = set_ends(jax.random.randint(seeds[2], (TOKENS, TOPK), 32, 256), jax.random.fold_in(seeds[2], 1), 32, 255).astype(jnp.int32)
    gate_weight = normal_values(seeds[3], (EXPERTS, D, FF), D ** -0.5, 0.09375, ((0, 128), (2, 2)))
    up_weight = normal_values(seeds[4], (EXPERTS, D, FF), D ** -0.5, 0.09375, ((0, 128), (2, 2)))
    down_weight = normal_values(seeds[5], (EXPERTS, FF, D), FF ** -0.5, 0.21875, ((0, 128), (1, 2)))
    return dict(tokens=tokens, expert_ids=expert_ids, gate_levels=gate_levels, gate_weight=gate_weight, up_weight=up_weight, down_weight=down_weight)


def expert_output(rows_in, w_gate, w_up, w_down):
    gate_values = jnp.dot(rows_in, w_gate, preferred_element_type=jnp.float32)
    up_values = jnp.dot(rows_in, w_up, preferred_element_type=jnp.float32)
    hidden = (jax.nn.silu(gate_values) * up_values).astype(jnp.bfloat16)
    group_cols = FF // N_TP
    summed = jnp.zeros((rows_in.shape[0], D), jnp.float32)
    for member in range(N_TP):
        first = member * group_cols
        part_value = jnp.dot(hidden[:, first:first + group_cols], w_down[first:first + group_cols], preferred_element_type=jnp.float32).astype(jnp.bfloat16)
        part_value = lax.optimization_barrier(part_value)
        summed = summed + part_value.astype(jnp.float32)
    return summed.astype(jnp.bfloat16)


def reference(tokens, expert_ids, gate_levels, gate_weight, up_weight, down_weight):
    per_block = TOK_DEV * TOPK
    slots_all = N_EP * CAP
    route_ids = expert_ids.reshape(N_EP, per_block).astype(jnp.int32)
    onehot = (route_ids[:, :, None] == jnp.arange(EXPERTS, dtype=jnp.int32)[None, None, :]).astype(jnp.int32)
    earlier = jnp.cumsum(onehot, axis=1) - onehot
    slot_rank = jnp.sum(earlier * onehot, axis=2).astype(jnp.int32)
    block_index = jnp.arange(N_EP, dtype=jnp.int32)[:, None]
    target = (route_ids * slots_all + block_index * CAP + slot_rank).reshape(-1).astype(jnp.int32)
    token_index = (jnp.arange(TOKENS * TOPK, dtype=jnp.int32) // TOPK).astype(jnp.int32)
    levels = gate_levels.astype(jnp.float32)
    weights = (levels / jnp.sum(levels, axis=1, keepdims=True)).reshape(-1)
    source_token = jnp.full((EXPERTS * slots_all,), TOKENS, jnp.int32).at[target].set(token_index).reshape(EXPERTS, slots_all)
    route_weight = jnp.zeros((EXPERTS * slots_all,), jnp.float32).at[target].set(weights).reshape(EXPERTS, slots_all)
    padded_tokens = jnp.concatenate([tokens, jnp.zeros((1, D), tokens.dtype)], axis=0)

    def per_expert(collected, inputs):
        rows_from, scale, w_gate, w_up, w_down = inputs
        produced = expert_output(padded_tokens[rows_from], w_gate, w_up, w_down)
        collected = collected.at[rows_from].add(scale[:, None] * produced.astype(jnp.float32))
        return collected, None

    collected, unused = lax.scan(per_expert, jnp.zeros((TOKENS + 1, D), jnp.float32), (source_token, route_weight, gate_weight, up_weight, down_weight))
    return collected[:TOKENS].astype(jnp.bfloat16)
```

```python
import jax
import jax.numpy as jnp
from jax import lax
from jax.sharding import Mesh, PartitionSpec as P

PLANE = (4, 4)
CHUNKS = 2
SWAP = [(0, 1), (1, 0)]


def swap(array):
    return lax.ppermute(array, "tp", SWAP)


def on_device(tokens, expert_ids, gate_levels, gate_weight, up_weight, down_weight):
    planes = lax.axis_size("z")
    plane_experts = lax.axis_size("y") * lax.axis_size("x")
    core = lax.axis_index("tp")
    tok_count, top_count = expert_ids.shape
    half_width = tokens.shape[1]
    experts_all = planes * plane_experts
    capacity = 3 * tok_count * top_count // (2 * experts_all)
    blocks = planes // 2
    my_tokens = blocks * tok_count
    my_slots = blocks * capacity
    width = half_width // CHUNKS

    meta = lax.all_gather(
        jnp.concatenate([expert_ids, gate_levels], axis=1), "z", axis=0, tiled=True
    )
    mine = lax.dynamic_slice_in_dim(meta, core * my_tokens, my_tokens, 0)
    ids, levels = mine[:, :top_count], mine[:, top_count:].astype(jnp.float32)
    weights = levels / jnp.sum(levels, axis=1, keepdims=True)
    first = lax.axis_index("z") * plane_experts
    plane_ids = first + jnp.arange(plane_experts, dtype=jnp.int32)
    hits = ids[None, :, :] == plane_ids[:, None, None]
    named = jnp.any(hits, axis=2)
    scale = jnp.sum(jnp.where(hits, weights[None, :, :], 0.0), axis=2)
    order = jnp.arange(tok_count)
    before = (order[:, None] < order[None, :]).astype(jnp.bfloat16)
    rank = jnp.einsum(
        "ebt,ts->ebs",
        named.reshape(plane_experts, blocks, tok_count).astype(jnp.bfloat16),
        before,
        preferred_element_type=jnp.float32,
    ).astype(jnp.int32)
    place = rank + capacity * jnp.arange(blocks, dtype=jnp.int32)[None, :, None]
    place = jnp.where(named, place.reshape(plane_experts, my_tokens), -1)
    fits = place[:, None, :] == jnp.arange(my_slots, dtype=jnp.int32)[None, :, None]
    rows = plane_experts * my_slots
    select = fits.astype(jnp.bfloat16).reshape(rows, my_tokens)
    mix = jnp.where(fits, scale[:, None, :], 0.0).astype(jnp.bfloat16).reshape(rows, my_tokens)

    w_gate = jnp.concatenate([gate_weight[0], swap(gate_weight[0])], axis=1)
    w_up = jnp.concatenate([up_weight[0], swap(up_weight[0])], axis=1)
    w_down = jnp.concatenate([down_weight[0], swap(down_weight[0])], axis=0)

    def both(array, index, axis):
        own = core * half_width + index * width
        other = (1 - core) * half_width + index * width
        return jnp.concatenate(
            [
                lax.dynamic_slice_in_dim(array, own, width, axis),
                lax.dynamic_slice_in_dim(array, other, width, axis),
            ],
            axis=axis,
        )

    gate_values = up_values = 0.0
    for index in range(CHUNKS):
        piece = tokens[:, index * width : (index + 1) * width]
        column = lax.all_gather(piece, "z", axis=0, tiled=True)
        keep = lax.dynamic_slice_in_dim(column, core * my_tokens, my_tokens, 0)
        give = lax.dynamic_slice_in_dim(column, (1 - core) * my_tokens, my_tokens, 0)
        features = jnp.concatenate([keep, swap(give)], axis=1)
        outgoing = jnp.dot(select, features, preferred_element_type=jnp.float32)
        outgoing = outgoing.astype(jnp.bfloat16).reshape(plane_experts, my_slots, 2 * width)
        arrived = lax.all_to_all(outgoing, ("y", "x"), split_axis=0, concat_axis=0, tiled=True)
        arrived = arrived.reshape(rows, 2 * width)
        gate_values += jnp.dot(
            arrived, both(w_gate, index, 0), preferred_element_type=jnp.float32
        )
        up_values += jnp.dot(arrived, both(w_up, index, 0), preferred_element_type=jnp.float32)
    hidden = (jax.nn.silu(gate_values) * up_values).astype(jnp.bfloat16)

    outputs = []
    for index in range(CHUNKS):
        produced = jnp.dot(hidden, both(w_down, index, 1), preferred_element_type=jnp.float32)
        produced = produced.astype(jnp.bfloat16).reshape(plane_experts, my_slots, 2 * width)
        returned = lax.all_to_all(produced, ("y", "x"), split_axis=0, concat_axis=0, tiled=True)
        returned = returned.reshape(rows, 2 * width)
        partial = lax.dot_general(
            mix, returned, (((0,), (0,)), ((), ())), preferred_element_type=jnp.float32
        ).astype(jnp.bfloat16)
        own, other = partial[:, :width], swap(partial[:, width:])
        column = jnp.concatenate(
            [jnp.where(core == 0, own, other), jnp.where(core == 0, other, own)], axis=0
        )
        outputs.append(lax.psum_scatter(column, "z", scatter_dimension=0, tiled=True))
    return jnp.concatenate(outputs, axis=1)


def solution(mesh):
    n_ep, n_tp = mesh.shape["ep"], mesh.shape["tp"]
    n_y, n_x = PLANE
    torus = Mesh(
        mesh.devices.reshape(n_ep // (n_y * n_x), n_y, n_x, n_tp), ("z", "y", "x", "tp")
    )
    ep = ("z", "y", "x")
    in_specs = (
        P(ep, "tp"),
        P(ep, None),
        P(ep, None),
        P(ep, None, "tp"),
        P(ep, None, "tp"),
        P(ep, "tp", None),
    )
    return jax.shard_map(
        on_device, mesh=torus, in_specs=in_specs, out_specs=P(ep, "tp"), check_vma=False
    )
```

```python
import jax
import jax.numpy as jnp
from jax import lax
from jax.sharding import Mesh, PartitionSpec as P

PLANE = (4, 4)
CUTS = (0, 16, 32, 48)


def swap(array):
    return lax.ppermute(array, "tp", [(0, 1), (1, 0)])


def around(array, step):
    planes = lax.axis_size("z")
    pairs = []
    for plane in range(planes):
        pairs.append((2 * plane, 2 * ((plane + step) % planes)))
        pairs.append((2 * plane + 1, 2 * ((plane - step) % planes) + 1))
    return lax.ppermute(array, ("z", "tp"), pairs)


def exchange(array):
    return lax.all_to_all(array, ("y", "x"), split_axis=0, concat_axis=0, tiled=True)


def on_device(tokens, expert_ids, gate_levels, gate_weight, up_weight, down_weight):
    planes = lax.axis_size("z")
    plane_experts = lax.axis_size("y") * lax.axis_size("x")
    core = lax.axis_index("tp")
    tok_count, top_count = expert_ids.shape
    half_width = tokens.shape[1]
    model_width = 2 * half_width
    capacity = 3 * tok_count * top_count // (2 * planes * plane_experts)
    far = planes // 2
    half_slots = capacity // 2
    starts = [0] + [half_slots + capacity * (k - 1) for k in range(1, far + 1)]
    ends = starts[1:] + [starts[-1] + half_slots]
    chunks = list(zip(CUTS[:-1], CUTS[1:]))

    routes = jnp.concatenate([expert_ids, gate_levels], axis=1).T.astype(jnp.bfloat16)
    routes = jnp.pad(routes, ((0, tok_count - 2 * top_count), (0, 128 - tok_count)))
    received = swap(tokens)
    low = jnp.where(core == 0, tokens, received)
    high = jnp.where(core == 0, received, tokens)
    blocks = [jnp.concatenate([low, high, routes], axis=1)]
    for k in range(far):
        blocks.append(around(blocks[k], 1))

    first = lax.axis_index("z") * plane_experts
    plane_ids = first + jnp.arange(plane_experts, dtype=jnp.int32)
    order = jnp.arange(tok_count)
    before = (order[:, None] < order[None, :]).astype(jnp.bfloat16)

    def places(k):
        table = blocks[k][: 2 * top_count, model_width : model_width + tok_count]
        ids = table[:top_count].astype(jnp.int32)
        levels = table[top_count:].astype(jnp.float32)
        weights = levels / jnp.sum(levels, axis=0, keepdims=True)
        hits = ids[None, :, :] == plane_ids[:, None, None]
        named = jnp.any(hits, axis=1)
        scale = jnp.sum(jnp.where(hits, weights[None, :, :], 0.0), axis=1)
        rank = jnp.dot(
            named.astype(jnp.bfloat16), before, preferred_element_type=jnp.float32
        ).astype(jnp.int32)
        if k in (0, far):
            rank = rank - core * half_slots
            named = named & (rank >= 0) & (rank < half_slots)
        return jnp.where(named, rank + starts[k], -1), scale

    placed = [places(k) for k in range(far + 1)]

    def within(k, chunk):
        return starts[k] < chunk[1] and chunk[0] < ends[k]

    def fits(k, chunk):
        slots = jnp.arange(chunk[0], chunk[1], dtype=jnp.int32)
        return placed[k][0][:, None, :] == slots[None, :, None]

    w_gate = jnp.concatenate([gate_weight[0], swap(gate_weight[0])], axis=1)
    w_up = jnp.concatenate([up_weight[0], swap(up_weight[0])], axis=1)
    w_down = jnp.concatenate([down_weight[0], swap(down_weight[0])], axis=0)

    arrivals = []
    for chunk in chunks:
        rows = plane_experts * (chunk[1] - chunk[0])
        outgoing = 0.0
        for k in range(far + 1):
            if within(k, chunk):
                select = fits(k, chunk).astype(jnp.bfloat16).reshape(rows, tok_count)
                outgoing += jnp.dot(
                    select, blocks[k][:, :model_width], preferred_element_type=jnp.float32
                )
        outgoing = outgoing.astype(jnp.bfloat16).reshape(plane_experts, -1, model_width)
        arrivals.append(exchange(outgoing))

    returns = [None] * len(chunks)
    for index in reversed(range(len(chunks))):
        arrived = arrivals[index].reshape(-1, model_width)
        gate_values = jnp.dot(arrived, w_gate, preferred_element_type=jnp.float32)
        up_values = jnp.dot(arrived, w_up, preferred_element_type=jnp.float32)
        hidden = (jax.nn.silu(gate_values) * up_values).astype(jnp.bfloat16)
        produced = jnp.dot(hidden, w_down, preferred_element_type=jnp.float32)
        produced = produced.astype(jnp.bfloat16).reshape(plane_experts, -1, model_width)
        returns[index] = exchange(produced).reshape(-1, model_width)

    total = 0.0
    for k in reversed(range(far + 1)):
        for index in reversed(range(len(chunks))):
            chunk = chunks[index]
            if within(k, chunk):
                mix = jnp.where(fits(k, chunk), placed[k][1][:, None, :], 0.0)
                mix = mix.astype(jnp.bfloat16).reshape(-1, tok_count)
                total += lax.dot_general(
                    mix,
                    returns[index],
                    (((0,), (0,)), ((), ())),
                    preferred_element_type=jnp.float32,
                )
        if k > 0:
            total = around(total.astype(jnp.bfloat16), -1).astype(jnp.float32)
    low, high = total[:, :half_width], total[:, half_width:]
    own = jnp.where(core == 0, low, high)
    other = jnp.where(core == 0, high, low).astype(jnp.bfloat16)
    return (own + swap(other).astype(jnp.float32)).astype(jnp.bfloat16)


def solution(mesh):
    n_ep, n_tp = mesh.shape["ep"], mesh.shape["tp"]
    n_y, n_x = PLANE
    torus = Mesh(
        mesh.devices.reshape(n_ep // (n_y * n_x), n_y, n_x, n_tp), ("z", "y", "x", "tp")
    )
    ep = ("z", "y", "x")
    in_specs = (
        P(ep, "tp"),
        P(ep, None),
        P(ep, None),
        P(ep, None, "tp"),
        P(ep, None, "tp"),
        P(ep, "tp", None),
    )
    return jax.shard_map(
        on_device, mesh=torus, in_specs=in_specs, out_specs=P(ep, "tp"), check_vma=False
    )
```

```python
import jax
import jax.numpy as jnp
from jax import lax
from jax.experimental import pallas as pl
from jax.experimental.pallas import tpu as pltpu
from jax.sharding import Mesh, PartitionSpec as P

PLANE = (4, 4)
CUTS = (0, 16, 24, 48)
TILE = 1024


def swap(array):
    return lax.ppermute(array, "tp", [(0, 1), (1, 0)])


def around(array, step):
    planes = lax.axis_size("z")
    pairs = []
    for plane in range(planes):
        pairs.append((2 * plane, 2 * ((plane + step) % planes)))
        pairs.append((2 * plane + 1, 2 * ((plane - step) % planes) + 1))
    return lax.ppermute(array, ("z", "tp"), pairs)


def expert_kernel(
    x, gate_a, gate_b, up_a, up_b, down_a, down_b, out,
    rows_in, into, out_of, rows_out, sums, hidden, into_sems, out_of_sems, done_sems,
):
    tiles, tile = into.shape[0], into.shape[1]
    half = gate_a.shape[1]
    units = 2 * half

    def inward(k):
        part = pl.ds(pl.multiple_of(k * tile, tile), tile)
        copies = [pltpu.make_async_copy(x.at[:, part], rows_in.at[k], into_sems.at[k, 4])]
        for j, weight in enumerate((gate_a, gate_b, up_a, up_b)):
            columns = into.at[k, :, pl.ds(j * half, half)]
            copies.append(pltpu.make_async_copy(weight.at[part, :], columns, into_sems.at[k, j]))
        return copies

    def outward(k):
        part = pl.ds(pl.multiple_of(k * tile, tile), tile)
        return [
            pltpu.make_async_copy(
                weight.at[:, part], out_of.at[k, pl.ds(j * half, half), :], out_of_sems.at[k, j]
            )
            for j, weight in enumerate((down_a, down_b))
        ]

    def result(k):
        part = pl.ds(pl.multiple_of(k * tile, tile), tile)
        return pltpu.make_async_copy(rows_out.at[k], out.at[:, part], done_sems.at[k])

    for k in range(tiles):
        for copy in inward(k):
            copy.start()
    for k in range(tiles):
        for copy in outward(k):
            copy.start()
    sums[...] = jnp.zeros_like(sums)

    @pl.loop(0, tiles)
    def _(k):
        for copy in inward(k):
            copy.wait()
        sums[...] += jnp.dot(rows_in[k], into[k], preferred_element_type=jnp.float32)

    gate = sums[:, :units]
    hidden[...] = (gate / (1.0 + jnp.exp(-gate)) * sums[:, units:]).astype(jnp.bfloat16)

    @pl.loop(0, tiles)
    def _(k):
        for copy in outward(k):
            copy.wait()
        product = jnp.dot(hidden[...], out_of[k], preferred_element_type=jnp.float32)
        rows_out[k] = product.astype(jnp.bfloat16)
        result(k).start()

    for k in range(tiles):
        result(k).wait()


def run_expert(x, gates, ups, downs):
    rows, width = x.shape
    half = gates[0].shape[1]
    tile = min(TILE, width)
    tiles = width // tile
    return pl.pallas_call(
        expert_kernel,
        in_specs=[pl.BlockSpec(memory_space=pl.ANY)] * 7,
        out_specs=pl.BlockSpec(memory_space=pl.ANY),
        out_shape=jax.ShapeDtypeStruct((rows, width), jnp.bfloat16),
        scratch_shapes=[
            pltpu.VMEM((tiles, rows, tile), jnp.bfloat16),
            pltpu.VMEM((tiles, tile, 4 * half), jnp.bfloat16),
            pltpu.VMEM((tiles, 2 * half, tile), jnp.bfloat16),
            pltpu.VMEM((tiles, rows, tile), jnp.bfloat16),
            pltpu.VMEM((rows, 4 * half), jnp.float32),
            pltpu.VMEM((rows, 2 * half), jnp.bfloat16),
            pltpu.SemaphoreType.DMA((tiles, 5)),
            pltpu.SemaphoreType.DMA((tiles, 2)),
            pltpu.SemaphoreType.DMA((tiles,)),
        ],
        compiler_params=pltpu.CompilerParams(vmem_limit_bytes=60 * 1024 * 1024),
    )(x, *gates, *ups, *downs)


def tied(array, *after):
    return lax.optimization_barrier((array, *after))[0] if after else array


def exchange(array):
    return lax.all_to_all(array, ("y", "x"), split_axis=0, concat_axis=0, tiled=True)


def on_device(tokens, expert_ids, gate_levels, gate_weight, up_weight, down_weight):
    planes = lax.axis_size("z")
    plane_experts = lax.axis_size("y") * lax.axis_size("x")
    core = lax.axis_index("tp")
    tok_count, top_count = expert_ids.shape
    half_width = tokens.shape[1]
    model_width = 2 * half_width
    capacity = 3 * tok_count * top_count // (2 * planes * plane_experts)
    far = planes // 2
    half_slots = capacity // 2
    starts = [0] + [half_slots + capacity * (k - 1) for k in range(1, far + 1)]
    ends = starts[1:] + [starts[-1] + half_slots]
    chunks = list(zip(CUTS[:-1], CUTS[1:]))

    routes = jnp.concatenate([expert_ids, gate_levels], axis=1).T.astype(jnp.bfloat16)
    routes = jnp.pad(routes, ((0, tok_count - 2 * top_count), (0, 128 - tok_count)))
    received = swap(tokens)
    low = jnp.where(core == 0, tokens, received)
    high = jnp.where(core == 0, received, tokens)
    blocks = [jnp.concatenate([low, high, routes], axis=1)]

    first = lax.axis_index("z") * plane_experts
    plane_ids = first + jnp.arange(plane_experts, dtype=jnp.int32)
    order = jnp.arange(tok_count)
    before = (order[:, None] < order[None, :]).astype(jnp.bfloat16)

    def places(k):
        table = blocks[k][: 2 * top_count, model_width : model_width + tok_count]
        ids = table[:top_count].astype(jnp.int32)
        levels = table[top_count:].astype(jnp.float32)
        weights = levels / jnp.sum(levels, axis=0, keepdims=True)
        hits = ids[None, :, :] == plane_ids[:, None, None]
        named = jnp.any(hits, axis=1)
        scale = jnp.sum(jnp.where(hits, weights[None, :, :], 0.0), axis=1)
        rank = jnp.dot(
            named.astype(jnp.bfloat16), before, preferred_element_type=jnp.float32
        ).astype(jnp.int32)
        if k in (0, far):
            rank = rank - core * half_slots
            named = named & (rank >= 0) & (rank < half_slots)
        return jnp.where(named, rank + starts[k], -1), scale

    placed = []

    def reach(k, *after):
        while len(placed) <= k:
            if placed:
                blocks.append(around(tied(blocks[-1], *after), 1))
            placed.append(places(len(placed)))

    def within(k, chunk):
        return starts[k] < chunk[1] and chunk[0] < ends[k]

    def fits(k, chunk):
        slots = jnp.arange(chunk[0], chunk[1], dtype=jnp.int32)
        return placed[k][0][:, None, :] == slots[None, :, None]

    def pair(weight):
        return weight, swap(weight)

    gates, ups, downs = pair(gate_weight[0]), pair(up_weight[0]), pair(down_weight[0])

    def selected(index):
        chunk = chunks[index]
        rows = plane_experts * (chunk[1] - chunk[0])
        outgoing = 0.0
        for k in range(far + 1):
            if within(k, chunk):
                select = fits(k, chunk).astype(jnp.bfloat16).reshape(rows, tok_count)
                outgoing += jnp.dot(
                    select, blocks[k][:, :model_width], preferred_element_type=jnp.float32
                )
        return outgoing.astype(jnp.bfloat16).reshape(plane_experts, -1, model_width)

    def expert(arrived):
        produced = run_expert(arrived.reshape(-1, model_width), gates, ups, downs)
        return produced.reshape(plane_experts, -1, model_width)

    def last_block(index):
        return max(k for k in range(far + 1) if within(k, chunks[index]))

    reach(last_block(0))
    outgoing = [selected(0)]
    reach(2)
    reach(3, outgoing[0])
    arrived = [exchange(outgoing[0])]
    for index in range(1, len(chunks)):
        reach(last_block(index), arrived[0], *outgoing)
        outgoing.append(selected(index))
        arrived.append(exchange(outgoing[index]))
    produced = []
    for index in range(len(chunks)):
        here = tied(arrived[index], *arrived[index + 1 : len(chunks) - 1])
        produced.append(expert(here))

    returns = [None] * len(chunks)
    before_it = tuple(produced[:-1])
    for index in reversed(range(len(chunks))):
        returns[index] = exchange(tied(produced[index], *before_it))
        before_it = (returns[index],)
    returns = [one.reshape(-1, model_width) for one in returns]

    total = 0.0
    for k in reversed(range(far + 1)):
        for index in reversed(range(len(chunks))):
            chunk = chunks[index]
            if within(k, chunk):
                mix = jnp.where(fits(k, chunk), placed[k][1][:, None, :], 0.0)
                mix = mix.astype(jnp.bfloat16).reshape(-1, tok_count)
                total += lax.dot_general(
                    mix,
                    returns[index],
                    (((0,), (0,)), ((), ())),
                    preferred_element_type=jnp.float32,
                )
        if k > 0:
            total = around(total.astype(jnp.bfloat16), -1).astype(jnp.float32)
    low, high = total[:, :half_width], total[:, half_width:]
    own = jnp.where(core == 0, low, high)
    other = jnp.where(core == 0, high, low).astype(jnp.bfloat16)
    return (own + swap(other).astype(jnp.float32)).astype(jnp.bfloat16)


def solution(mesh):
    n_ep, n_tp = mesh.shape["ep"], mesh.shape["tp"]
    n_y, n_x = PLANE
    torus = Mesh(
        mesh.devices.reshape(n_ep // (n_y * n_x), n_y, n_x, n_tp), ("z", "y", "x", "tp")
    )
    ep = ("z", "y", "x")
    in_specs = (
        P(ep, "tp"),
        P(ep, None),
        P(ep, None),
        P(ep, None, "tp"),
        P(ep, None, "tp"),
        P(ep, "tp", None),
    )
    return jax.shard_map(
        on_device, mesh=torus, in_specs=in_specs, out_specs=P(ep, "tp"), check_vma=False
    )
```

```python
import functools

import jax
import jax.numpy as jnp
from jax import lax
from jax.experimental import pallas as pl
from jax.experimental.pallas import tpu as pltpu
from jax.sharding import Mesh, PartitionSpec as P

PLANE = (4, 4)
CHUNKS = ((0,), (1,), (2,), (3, 4))
TILES = 4
AFTER_SELECTED = {3: 1}
WITH_ARRIVED = {1: 0, 3: 1, 4: 2}


def swap(array):
    return lax.ppermute(array, "tp", [(0, 1), (1, 0)])


def around(array, step):
    planes = lax.axis_size("z")
    pairs = []
    for plane in range(planes):
        pairs.append((2 * plane, 2 * ((plane + step) % planes)))
        pairs.append((2 * plane + 1, 2 * ((plane - step) % planes) + 1))
    return lax.ppermute(array, ("z", "tp"), pairs)


def expert_kernel(pieces, *refs):
    count = len(pieces)
    inputs, refs = refs[:count], refs[count:]
    gate_a, gate_b, up_a, up_b, down_a, down_b = refs[:6]
    outputs, refs = refs[6 : 6 + count], refs[6 + count :]
    rows_in, into, out_of, rows_out, sums, hidden, in_sems, into_sems, out_of_sems, done_sems = refs
    tiles, tile = into.shape[0], into.shape[1]
    half = gate_a.shape[1]
    units = 2 * half
    spots, first = [], 0
    for array, (groups, rows) in enumerate(pieces):
        for group in range(groups):
            spots.append((array, group, pl.ds(first, rows)))
            first += rows

    def inward(k):
        part = pl.ds(pl.multiple_of(k * tile, tile), tile)
        copies = []
        for j, (array, group, spot) in enumerate(spots):
            source = inputs[array].at[group, k]
            copies.append(pltpu.make_async_copy(source, rows_in.at[k, spot], in_sems.at[k, j]))
        for j, weight in enumerate((gate_a, gate_b, up_a, up_b)):
            columns = into.at[k, :, pl.ds(j * half, half)]
            copies.append(pltpu.make_async_copy(weight.at[part, :], columns, into_sems.at[k, j]))
        return copies

    def outward(k):
        part = pl.ds(pl.multiple_of(k * tile, tile), tile)
        return [
            pltpu.make_async_copy(
                weight.at[:, part], out_of.at[k, pl.ds(j * half, half), :], out_of_sems.at[k, j]
            )
            for j, weight in enumerate((down_a, down_b))
        ]

    def results(k):
        return [
            pltpu.make_async_copy(
                rows_out.at[k, spot], outputs[array].at[group, k], done_sems.at[k, j]
            )
            for j, (array, group, spot) in enumerate(spots)
        ]

    for k in range(tiles):
        for copy in inward(k):
            copy.start()
    for k in range(tiles):
        for copy in outward(k):
            copy.start()
    sums[...] = jnp.zeros_like(sums)

    @pl.loop(0, tiles)
    def _(k):
        for copy in inward(k):
            copy.wait()
        sums[...] += jnp.dot(rows_in[k], into[k], preferred_element_type=jnp.float32)

    gate = sums[:, :units]
    hidden[...] = (gate / (1.0 + jnp.exp(-gate)) * sums[:, units:]).astype(jnp.bfloat16)

    @pl.loop(0, tiles)
    def _(k):
        for copy in outward(k):
            copy.wait()
        product = jnp.dot(hidden[...], out_of[k], preferred_element_type=jnp.float32)
        rows_out[k] = product.astype(jnp.bfloat16)
        for copy in results(k):
            copy.start()

    for k in range(tiles):
        for copy in results(k):
            copy.wait()


def run_expert(arrays, gates, ups, downs):
    tiles, tile = arrays[0].shape[1], arrays[0].shape[3]
    pieces = [(array.shape[0], array.shape[2]) for array in arrays]
    rows = sum(groups * held for groups, held in pieces)
    spots = sum(groups for groups, held in pieces)
    half = gates[0].shape[1]
    return pl.pallas_call(
        functools.partial(expert_kernel, pieces),
        in_specs=[pl.BlockSpec(memory_space=pl.ANY)] * (len(arrays) + 6),
        out_specs=[pl.BlockSpec(memory_space=pl.ANY)] * len(arrays),
        out_shape=[jax.ShapeDtypeStruct(array.shape, jnp.bfloat16) for array in arrays],
        scratch_shapes=[
            pltpu.VMEM((tiles, rows, tile), jnp.bfloat16),
            pltpu.VMEM((tiles, tile, 4 * half), jnp.bfloat16),
            pltpu.VMEM((tiles, 2 * half, tile), jnp.bfloat16),
            pltpu.VMEM((tiles, rows, tile), jnp.bfloat16),
            pltpu.VMEM((rows, 4 * half), jnp.float32),
            pltpu.VMEM((rows, 2 * half), jnp.bfloat16),
            pltpu.SemaphoreType.DMA((tiles, spots)),
            pltpu.SemaphoreType.DMA((tiles, 4)),
            pltpu.SemaphoreType.DMA((tiles, 2)),
            pltpu.SemaphoreType.DMA((tiles, spots)),
        ],
        compiler_params=pltpu.CompilerParams(vmem_limit_bytes=60 * 1024 * 1024),
    )(*arrays, *gates, *ups, *downs)


def tied(array, *after):
    return lax.optimization_barrier((array, *after))[0] if after else array


def exchange(array):
    return lax.all_to_all(array, ("y", "x"), split_axis=0, concat_axis=0, tiled=True)


def on_device(tokens, expert_ids, gate_levels, gate_weight, up_weight, down_weight):
    planes = lax.axis_size("z")
    plane_experts = lax.axis_size("y") * lax.axis_size("x")
    core = lax.axis_index("tp")
    tok_count, top_count = expert_ids.shape
    half_width = tokens.shape[1]
    tile = 2 * half_width // TILES
    capacity = 3 * tok_count * top_count // (2 * planes * plane_experts)
    far = planes // 2
    slots = [capacity // 2 if k in (0, far) else capacity for k in range(far + 1)]
    group = plane_experts // 2
    tall = TILES * tok_count

    routes = jnp.concatenate([expert_ids, gate_levels], axis=1).T.astype(jnp.bfloat16)
    routes = jnp.pad(routes, ((0, 0), (0, tile - tok_count)))
    received = swap(tokens)
    low = jnp.where(core == 0, tokens, received)
    high = jnp.where(core == 0, received, tokens)
    parts = [
        array[:, first : first + tile]
        for array in (low, high)
        for first in range(0, half_width, tile)
    ]
    blocks = [jnp.concatenate([*parts, routes], axis=0)]

    first = lax.axis_index("z") * plane_experts
    plane_ids = first + jnp.arange(plane_experts, dtype=jnp.int32)
    order = jnp.arange(tok_count)
    before = (order[:, None] < order[None, :]).astype(jnp.bfloat16)

    def places(k):
        table = blocks[k][tall:, :tok_count]
        ids = table[:top_count].astype(jnp.int32)
        levels = table[top_count:].astype(jnp.float32)
        weights = levels / jnp.sum(levels, axis=0, keepdims=True)
        hits = ids[None, :, :] == plane_ids[:, None, None]
        named = jnp.any(hits, axis=1)
        scale = jnp.sum(jnp.where(hits, weights[None, :, :], 0.0), axis=1)
        rank = jnp.dot(
            named.astype(jnp.bfloat16), before, preferred_element_type=jnp.float32
        ).astype(jnp.int32)
        if k in (0, far):
            rank = rank - core * slots[k]
            named = named & (rank >= 0) & (rank < slots[k])
        return jnp.where(named, rank, -TILES * planes * capacity), scale

    placed = []

    def fits(k, chunk):
        held = sum(slots[j] for j in chunk)
        skipped = sum(slots[j] for j in chunk if j < k)
        starts = skipped + held * jnp.arange(TILES, dtype=jnp.int32)
        wanted = placed[k][0][:, None, :] + starts[None, :, None]
        rows = jnp.arange(TILES * held, dtype=jnp.int32)
        return rows[None, :, None, None] == wanted[:, None, :, :]

    def pair(weight):
        return weight, swap(weight)

    gates, ups, downs = pair(gate_weight[0]), pair(up_weight[0]), pair(down_weight[0])

    def selected(chunk):
        outgoing = 0.0
        for k in chunk:
            select = fits(k, chunk).astype(jnp.bfloat16).reshape(-1, tall)
            outgoing += jnp.dot(select, blocks[k][:tall], preferred_element_type=jnp.float32)
        return outgoing.astype(jnp.bfloat16).reshape(plane_experts, -1, tile)

    def turn(chunk):
        held = sum(slots[j] for j in chunk)
        row = jnp.arange(TILES * group * held, dtype=jnp.int32)
        source, rest = row // (TILES * held), row % (TILES * held)
        goal = (rest // held) * (group * held) + source * held + rest % held
        return (row[:, None] == goal[None, :]).astype(jnp.bfloat16)

    def grouped(array, chunk):
        array = array.reshape(plane_experts // group, -1, tile)
        array = jnp.einsum(
            "rc,gcd->grd", turn(chunk), array, preferred_element_type=jnp.float32
        )
        return array.astype(jnp.bfloat16).reshape(plane_experts // group, TILES, -1, tile)

    def ungrouped(array, chunk):
        array = array.reshape(plane_experts // group, -1, tile)
        array = jnp.einsum(
            "rc,grd->gcd", turn(chunk), array, preferred_element_type=jnp.float32
        )
        return array.astype(jnp.bfloat16).reshape(plane_experts, -1, tile)

    outgoing, arrived = [], []
    for index, chunk in enumerate(CHUNKS):
        for k in chunk:
            if k > 0:
                after = [outgoing[AFTER_SELECTED[k]]] if k in AFTER_SELECTED else []
                coming = around(tied(blocks[-1], *after), 1)
                if k in WITH_ARRIVED:
                    there = WITH_ARRIVED[k]
                    coming, arrived[there] = lax.optimization_barrier((coming, arrived[there]))
                blocks.append(coming)
            placed.append(places(k))
        outgoing.append(selected(chunk))
        arrived.append(exchange(outgoing[index]))

    last = len(CHUNKS) - 1
    early = [grouped(tied(arrived[i], *arrived[i + 1 : last]), CHUNKS[i]) for i in range(last)]
    produced = list(run_expert(early, gates, ups, downs))
    produced = [ungrouped(array, chunk) for array, chunk in zip(produced, CHUNKS)]
    late = run_expert([grouped(arrived[last], CHUNKS[last])], gates, ups, downs)
    produced.append(ungrouped(late[0], CHUNKS[last]))

    total = 0.0
    before_it = tuple(produced[:-1])
    for index in reversed(range(len(CHUNKS))):
        chunk = CHUNKS[index]
        returned = exchange(tied(produced[index], *before_it))
        before_it = (returned,)
        returned = returned.reshape(-1, tile)
        for k in reversed(chunk):
            mix = jnp.where(fits(k, chunk), placed[k][1][:, None, None, :], 0.0)
            total += lax.dot_general(
                mix.astype(jnp.bfloat16).reshape(-1, tall),
                returned,
                (((0,), (0,)), ((), ())),
                preferred_element_type=jnp.float32,
            )
            if k > 0:
                total = around(total.astype(jnp.bfloat16), -1).astype(jnp.float32)
    low, high = total[: tall // 2], total[tall // 2 :]
    own = jnp.where(core == 0, low, high)
    other = jnp.where(core == 0, high, low).astype(jnp.bfloat16)
    mixed = (own + swap(other).astype(jnp.float32)).astype(jnp.bfloat16)
    return jnp.concatenate(jnp.split(mixed, TILES // 2, axis=0), axis=1)


def solution(mesh):
    n_ep, n_tp = mesh.shape["ep"], mesh.shape["tp"]
    n_y, n_x = PLANE
    torus = Mesh(
        mesh.devices.reshape(n_ep // (n_y * n_x), n_y, n_x, n_tp), ("z", "y", "x", "tp")
    )
    ep = ("z", "y", "x")
    in_specs = (
        P(ep, "tp"),
        P(ep, None),
        P(ep, None),
        P(ep, None, "tp"),
        P(ep, None, "tp"),
        P(ep, "tp", None),
    )
    return jax.shard_map(
        on_device, mesh=torus, in_specs=in_specs, out_specs=P(ep, "tp"), check_vma=False
    )
```

```python
import jax
import jax.numpy as jnp
from jax import lax
from jax.experimental import pallas as pl
from jax.experimental.pallas import tpu as pltpu
from jax.sharding import Mesh, PartitionSpec as P

PLANE = (4, 4)
CUTS = (0, 16, 24, 48)
TILE = 1024


def swap(array):
    return lax.ppermute(array, "tp", [(0, 1), (1, 0)])


def around(array, step):
    planes = lax.axis_size("z")
    pairs = []
    for plane in range(planes):
        pairs.append((2 * plane, 2 * ((plane + step) % planes)))
        pairs.append((2 * plane + 1, 2 * ((plane - step) % planes) + 1))
    return lax.ppermute(array, ("z", "tp"), pairs)


def expert_kernel(
    x, gate_a, gate_b, up_a, up_b, down_a, down_b, out,
    rows_in, into, out_of, rows_out, sums, hidden, into_sems, out_of_sems, done_sems,
):
    tiles, tile = into.shape[0], into.shape[1]
    half = gate_a.shape[1]
    units = 2 * half

    def inward(k):
        part = pl.ds(pl.multiple_of(k * tile, tile), tile)
        copies = [pltpu.make_async_copy(x.at[:, part], rows_in.at[k], into_sems.at[k, 4])]
        for j, weight in enumerate((gate_a, gate_b, up_a, up_b)):
            columns = into.at[k, :, pl.ds(j * half, half)]
            copies.append(pltpu.make_async_copy(weight.at[part, :], columns, into_sems.at[k, j]))
        return copies

    def outward(k):
        part = pl.ds(pl.multiple_of(k * tile, tile), tile)
        return [
            pltpu.make_async_copy(
                weight.at[:, part], out_of.at[k, pl.ds(j * half, half), :], out_of_sems.at[k, j]
            )
            for j, weight in enumerate((down_a, down_b))
        ]

    def result(k):
        part = pl.ds(pl.multiple_of(k * tile, tile), tile)
        return pltpu.make_async_copy(rows_out.at[k], out.at[:, part], done_sems.at[k])

    for k in range(tiles):
        for copy in inward(k):
            copy.start()
    for k in range(tiles):
        for copy in outward(k):
            copy.start()
    sums[...] = jnp.zeros_like(sums)

    @pl.loop(0, tiles)
    def _(k):
        for copy in inward(k):
            copy.wait()
        sums[...] += jnp.dot(rows_in[k], into[k], preferred_element_type=jnp.float32)

    gate = sums[:, :units]
    hidden[...] = (gate / (1.0 + jnp.exp(-gate)) * sums[:, units:]).astype(jnp.bfloat16)

    @pl.loop(0, tiles)
    def _(k):
        for copy in outward(k):
            copy.wait()
        product = jnp.dot(hidden[...], out_of[k], preferred_element_type=jnp.float32)
        rows_out[k] = product.astype(jnp.bfloat16)
        result(k).start()

    for k in range(tiles):
        result(k).wait()


def run_expert(x, gates, ups, downs):
    rows, width = x.shape
    half = gates[0].shape[1]
    tile = min(TILE, width)
    tiles = width // tile
    return pl.pallas_call(
        expert_kernel,
        in_specs=[pl.BlockSpec(memory_space=pl.ANY)] * 7,
        out_specs=pl.BlockSpec(memory_space=pl.ANY),
        out_shape=jax.ShapeDtypeStruct((rows, width), jnp.bfloat16),
        scratch_shapes=[
            pltpu.VMEM((tiles, rows, tile), jnp.bfloat16),
            pltpu.VMEM((tiles, tile, 4 * half), jnp.bfloat16),
            pltpu.VMEM((tiles, 2 * half, tile), jnp.bfloat16),
            pltpu.VMEM((tiles, rows, tile), jnp.bfloat16),
            pltpu.VMEM((rows, 4 * half), jnp.float32),
            pltpu.VMEM((rows, 2 * half), jnp.bfloat16),
            pltpu.SemaphoreType.DMA((tiles, 5)),
            pltpu.SemaphoreType.DMA((tiles, 2)),
            pltpu.SemaphoreType.DMA((tiles,)),
        ],
        compiler_params=pltpu.CompilerParams(vmem_limit_bytes=60 * 1024 * 1024),
    )(x, *gates, *ups, *downs)


def tied(array, *after):
    return lax.optimization_barrier((array, *after))[0] if after else array


def exchange(array):
    return lax.all_to_all(array, ("y", "x"), split_axis=0, concat_axis=0, tiled=True)


def on_device(tokens, expert_ids, gate_levels, gate_weight, up_weight, down_weight):
    planes = lax.axis_size("z")
    plane_experts = lax.axis_size("y") * lax.axis_size("x")
    core = lax.axis_index("tp")
    tok_count, top_count = expert_ids.shape
    half_width = tokens.shape[1]
    model_width = 2 * half_width
    capacity = 3 * tok_count * top_count // (2 * planes * plane_experts)
    far = planes // 2
    half_slots = capacity // 2
    starts = [0] + [half_slots + capacity * (k - 1) for k in range(1, far + 1)]
    ends = starts[1:] + [starts[-1] + half_slots]
    chunks = list(zip(CUTS[:-1], CUTS[1:]))

    routes = jnp.concatenate([expert_ids, gate_levels], axis=1).T.astype(jnp.bfloat16)
    routes = jnp.pad(routes, ((0, tok_count - 2 * top_count), (0, 128 - tok_count)))
    received = swap(tokens)
    low = jnp.where(core == 0, tokens, received)
    high = jnp.where(core == 0, received, tokens)
    blocks = [jnp.concatenate([low, high, routes], axis=1)]

    first = lax.axis_index("z") * plane_experts
    plane_ids = first + jnp.arange(plane_experts, dtype=jnp.int32)
    order = jnp.arange(tok_count)
    before = (order[:, None] < order[None, :]).astype(jnp.bfloat16)

    def places(k):
        table = blocks[k][: 2 * top_count, model_width : model_width + tok_count]
        ids = table[:top_count].astype(jnp.int32)
        levels = table[top_count:].astype(jnp.float32)
        weights = levels / jnp.sum(levels, axis=0, keepdims=True)
        hits = ids[None, :, :] == plane_ids[:, None, None]
        named = jnp.any(hits, axis=1)
        scale = jnp.sum(jnp.where(hits, weights[None, :, :], 0.0), axis=1)
        rank = jnp.dot(
            named.astype(jnp.bfloat16), before, preferred_element_type=jnp.float32
        ).astype(jnp.int32)
        if k in (0, far):
            rank = rank - core * half_slots
            named = named & (rank >= 0) & (rank < half_slots)
        return jnp.where(named, rank + starts[k], -1), scale

    placed = []

    def reach(k, *after):
        while len(placed) <= k:
            if placed:
                blocks.append(around(tied(blocks[-1], *after), 1))
            placed.append(places(len(placed)))

    def within(k, chunk):
        return starts[k] < chunk[1] and chunk[0] < ends[k]

    def fits(k, chunk):
        slots = jnp.arange(chunk[0], chunk[1], dtype=jnp.int32)
        return placed[k][0][:, None, :] == slots[None, :, None]

    def pair(weight):
        return weight, swap(weight)

    gates, ups, downs = pair(gate_weight[0]), pair(up_weight[0]), pair(down_weight[0])

    def selected(index):
        chunk = chunks[index]
        rows = plane_experts * (chunk[1] - chunk[0])
        outgoing = 0.0
        for k in range(far + 1):
            if within(k, chunk):
                select = fits(k, chunk).astype(jnp.bfloat16).reshape(rows, tok_count)
                outgoing += jnp.dot(
                    select, blocks[k][:, :model_width], preferred_element_type=jnp.float32
                )
        return outgoing.astype(jnp.bfloat16).reshape(plane_experts, -1, model_width)

    def expert(arrived):
        produced = run_expert(arrived.reshape(-1, model_width), gates, ups, downs)
        return produced.reshape(plane_experts, -1, model_width)

    def last_block(index):
        return max(k for k in range(far + 1) if within(k, chunks[index]))

    reach(last_block(0))
    outgoing = [selected(0)]
    reach(2)
    reach(3, outgoing[0])
    arrived = [exchange(outgoing[0])]
    for index in range(1, len(chunks)):
        reach(last_block(index), arrived[0], *outgoing)
        outgoing.append(selected(index))
        arrived.append(exchange(outgoing[index]))
    produced = []
    for index in range(len(chunks)):
        here = tied(arrived[index], *arrived[index + 1 : len(chunks) - 1])
        produced.append(expert(here))

    returns = [None] * len(chunks)
    before_it = (*produced[:-1], arrived[-1])
    for index in (1, 2, 0):
        returns[index] = exchange(tied(produced[index], *before_it))
        before_it = (returns[index],)
    returns = [one.reshape(-1, model_width) for one in returns]

    totals = [0.0, 0.0]
    for k in reversed(range(far + 1)):
        for index in reversed(range(len(chunks))):
            chunk = chunks[index]
            if within(k, chunk):
                mix = jnp.where(fits(k, chunk), placed[k][1][:, None, :], 0.0)
                mix = mix.astype(jnp.bfloat16).reshape(-1, tok_count)
                for half in range(2):
                    totals[half] += lax.dot_general(
                        mix,
                        returns[index][:, half * half_width : (half + 1) * half_width],
                        (((0,), (0,)), ((), ())),
                        preferred_element_type=jnp.float32,
                    )
        if k > 0:
            totals = [
                around(total.astype(jnp.bfloat16), -1).astype(jnp.float32) for total in totals
            ]
    low, high = totals
    own = jnp.where(core == 0, low, high)
    other = jnp.where(core == 0, high, low).astype(jnp.bfloat16)
    return (own + swap(other).astype(jnp.float32)).astype(jnp.bfloat16)


def solution(mesh):
    n_ep, n_tp = mesh.shape["ep"], mesh.shape["tp"]
    n_y, n_x = PLANE
    torus = Mesh(
        mesh.devices.reshape(n_ep // (n_y * n_x), n_y, n_x, n_tp), ("z", "y", "x", "tp")
    )
    ep = ("z", "y", "x")
    in_specs = (
        P(ep, "tp"),
        P(ep, None),
        P(ep, None),
        P(ep, None, "tp"),
        P(ep, None, "tp"),
        P(ep, "tp", None),
    )
    return jax.shard_map(
        on_device, mesh=torus, in_specs=in_specs, out_specs=P(ep, "tp"), check_vma=False
    )
```

```python
import jax
import jax.numpy as jnp
from jax import lax
from jax.experimental import pallas as pl
from jax.experimental.pallas import tpu as pltpu
from jax.sharding import Mesh, PartitionSpec as P

PLANE = (4, 4)
CUTS = (0, 16, 24, 48)
TILE = 1024


def swap(array):
    return lax.ppermute(array, "tp", [(0, 1), (1, 0)])


def around(array, step):
    planes = lax.axis_size("z")
    pairs = []
    for plane in range(planes):
        pairs.append((2 * plane, 2 * ((plane + step) % planes)))
        pairs.append((2 * plane + 1, 2 * ((plane - step) % planes) + 1))
    return lax.ppermute(array, ("z", "tp"), pairs)


def expert_kernel(
    x, gate_a, gate_b, up_a, up_b, down_a, down_b, out,
    rows_in, into, out_of, rows_out, sums, hidden, into_sems, out_of_sems, done_sems,
):
    tiles, tile = into.shape[0], into.shape[1]
    half = gate_a.shape[1]
    units = 2 * half

    def inward(k):
        part = pl.ds(pl.multiple_of(k * tile, tile), tile)
        copies = [pltpu.make_async_copy(x.at[:, part], rows_in.at[k], into_sems.at[k, 4])]
        for j, weight in enumerate((gate_a, gate_b, up_a, up_b)):
            columns = into.at[k, :, pl.ds(j * half, half)]
            copies.append(pltpu.make_async_copy(weight.at[part, :], columns, into_sems.at[k, j]))
        return copies

    def outward(k):
        column = lax.rem(k + lax.axis_index("tp") * (tiles // 2), tiles)
        part = pl.ds(pl.multiple_of(column * tile, tile), tile)
        return [
            pltpu.make_async_copy(
                weight.at[:, part], out_of.at[k, pl.ds(j * half, half), :], out_of_sems.at[k, j]
            )
            for j, weight in enumerate((down_a, down_b))
        ]

    def result(k):
        part = pl.ds(pl.multiple_of(k * tile, tile), tile)
        return pltpu.make_async_copy(rows_out.at[k], out.at[:, part], done_sems.at[k])

    for k in range(tiles):
        for copy in inward(k):
            copy.start()
    for k in range(tiles):
        for copy in outward(k):
            copy.start()
    sums[...] = jnp.zeros_like(sums)

    @pl.loop(0, tiles)
    def _(k):
        for copy in inward(k):
            copy.wait()
        sums[...] += jnp.dot(rows_in[k], into[k], preferred_element_type=jnp.float32)

    gate = sums[:, :units]
    hidden[...] = (gate / (1.0 + jnp.exp(-gate)) * sums[:, units:]).astype(jnp.bfloat16)

    @pl.loop(0, tiles)
    def _(k):
        for copy in outward(k):
            copy.wait()
        product = jnp.dot(hidden[...], out_of[k], preferred_element_type=jnp.float32)
        rows_out[k] = product.astype(jnp.bfloat16)
        result(k).start()

    for k in range(tiles):
        result(k).wait()


def run_expert(x, gates, ups, downs):
    rows, width = x.shape
    half = gates[0].shape[1]
    tile = min(TILE, width)
    tiles = width // tile
    return pl.pallas_call(
        expert_kernel,
        in_specs=[pl.BlockSpec(memory_space=pl.ANY)] * 7,
        out_specs=pl.BlockSpec(memory_space=pl.ANY),
        out_shape=jax.ShapeDtypeStruct((rows, width), jnp.bfloat16),
        scratch_shapes=[
            pltpu.VMEM((tiles, rows, tile), jnp.bfloat16),
            pltpu.VMEM((tiles, tile, 4 * half), jnp.bfloat16),
            pltpu.VMEM((tiles, 2 * half, tile), jnp.bfloat16),
            pltpu.VMEM((tiles, rows, tile), jnp.bfloat16),
            pltpu.VMEM((rows, 4 * half), jnp.float32),
            pltpu.VMEM((rows, 2 * half), jnp.bfloat16),
            pltpu.SemaphoreType.DMA((tiles, 5)),
            pltpu.SemaphoreType.DMA((tiles, 2)),
            pltpu.SemaphoreType.DMA((tiles,)),
        ],
        compiler_params=pltpu.CompilerParams(vmem_limit_bytes=60 * 1024 * 1024),
    )(x, *gates, *ups, *downs)


def tied(array, *after):
    return lax.optimization_barrier((array, *after))[0] if after else array


def exchange(array):
    return lax.all_to_all(array, ("y", "x"), split_axis=0, concat_axis=0, tiled=True)


def on_device(tokens, expert_ids, gate_levels, gate_weight, up_weight, down_weight):
    planes = lax.axis_size("z")
    plane_experts = lax.axis_size("y") * lax.axis_size("x")
    core = lax.axis_index("tp")
    tok_count, top_count = expert_ids.shape
    half_width = tokens.shape[1]
    model_width = 2 * half_width
    capacity = 3 * tok_count * top_count // (2 * planes * plane_experts)
    far = planes // 2
    half_slots = capacity // 2
    starts = [0] + [half_slots + capacity * (k - 1) for k in range(1, far + 1)]
    ends = starts[1:] + [starts[-1] + half_slots]
    chunks = list(zip(CUTS[:-1], CUTS[1:]))

    routes = jnp.concatenate([expert_ids, gate_levels], axis=1).T.astype(jnp.bfloat16)
    routes = jnp.pad(routes, ((0, tok_count - 2 * top_count), (0, 128 - tok_count)))
    received = swap(tokens)
    low = jnp.where(core == 0, tokens, received)
    high = jnp.where(core == 0, received, tokens)
    blocks = [jnp.concatenate([low, high, routes], axis=1)]

    first = lax.axis_index("z") * plane_experts
    plane_ids = first + jnp.arange(plane_experts, dtype=jnp.int32)
    order = jnp.arange(tok_count)
    before = (order[:, None] < order[None, :]).astype(jnp.bfloat16)

    def places(k):
        table = blocks[k][: 2 * top_count, model_width : model_width + tok_count]
        ids = table[:top_count].astype(jnp.int32)
        levels = table[top_count:].astype(jnp.float32)
        weights = levels / jnp.sum(levels, axis=0, keepdims=True)
        hits = ids[None, :, :] == plane_ids[:, None, None]
        named = jnp.any(hits, axis=1)
        scale = jnp.sum(jnp.where(hits, weights[None, :, :], 0.0), axis=1)
        rank = jnp.dot(
            named.astype(jnp.bfloat16), before, preferred_element_type=jnp.float32
        ).astype(jnp.int32)
        if k in (0, far):
            rank = rank - core * half_slots
            named = named & (rank >= 0) & (rank < half_slots)
        return jnp.where(named, rank + starts[k], -1), scale

    placed = []

    def reach(k, *after):
        while len(placed) <= k:
            if placed:
                blocks.append(around(tied(blocks[-1], *after), 1))
            placed.append(places(len(placed)))

    def within(k, chunk):
        return starts[k] < chunk[1] and chunk[0] < ends[k]

    def fits(k, chunk):
        slots = jnp.arange(chunk[0], chunk[1], dtype=jnp.int32)
        return placed[k][0][:, None, :] == slots[None, :, None]

    def pair(weight):
        return weight, swap(weight)

    gates, ups, downs = pair(gate_weight[0]), pair(up_weight[0]), pair(down_weight[0])

    def selected(index):
        chunk = chunks[index]
        rows = plane_experts * (chunk[1] - chunk[0])
        outgoing = 0.0
        for k in range(far + 1):
            if within(k, chunk):
                select = fits(k, chunk).astype(jnp.bfloat16).reshape(rows, tok_count)
                outgoing += jnp.dot(
                    select, blocks[k][:, :model_width], preferred_element_type=jnp.float32
                )
        return outgoing.astype(jnp.bfloat16).reshape(plane_experts, -1, model_width)

    def expert(arrived):
        produced = run_expert(arrived.reshape(-1, model_width), gates, ups, downs)
        return produced.reshape(plane_experts, -1, model_width)

    def last_block(index):
        return max(k for k in range(far + 1) if within(k, chunks[index]))

    reach(last_block(0))
    outgoing = [selected(0)]
    reach(2)
    reach(3, outgoing[0])
    arrived = [exchange(outgoing[0])]
    for index in range(1, len(chunks)):
        reach(last_block(index), arrived[0], *outgoing)
        outgoing.append(selected(index))
        arrived.append(exchange(outgoing[index]))
    produced = []
    for index in range(len(chunks)):
        here = tied(arrived[index], *arrived[index + 1 : len(chunks) - 1])
        produced.append(expert(here))

    returns = [None] * len(chunks)
    before_it = (*produced[:-1], arrived[-1])
    for index in (1, 2, 0):
        returns[index] = exchange(tied(produced[index], *before_it))
        before_it = (returns[index],)
    returns = [one.reshape(-1, model_width) for one in returns]

    totals = [0.0, 0.0]
    for k in reversed(range(far + 1)):
        for index in reversed(range(len(chunks))):
            chunk = chunks[index]
            if within(k, chunk):
                mix = jnp.where(fits(k, chunk), placed[k][1][:, None, :], 0.0)
                mix = mix.astype(jnp.bfloat16).reshape(-1, tok_count)
                for half in range(2):
                    totals[half] += lax.dot_general(
                        mix,
                        returns[index][:, half * half_width : (half + 1) * half_width],
                        (((0,), (0,)), ((), ())),
                        preferred_element_type=jnp.float32,
                    )
        if k > 0:
            kept, given = [total.astype(jnp.bfloat16) for total in totals]
            kept = tied(kept, given)
            given = around(given, -1).astype(jnp.float32)
            kept = around(kept, -1).astype(jnp.float32)
            totals = [kept, given]
    kept, given = totals
    given = swap(given.astype(jnp.bfloat16)).astype(jnp.float32)
    return (kept + given).astype(jnp.bfloat16)


def solution(mesh):
    n_ep, n_tp = mesh.shape["ep"], mesh.shape["tp"]
    n_y, n_x = PLANE
    torus = Mesh(
        mesh.devices.reshape(n_ep // (n_y * n_x), n_y, n_x, n_tp), ("z", "y", "x", "tp")
    )
    ep = ("z", "y", "x")
    in_specs = (
        P(ep, "tp"),
        P(ep, None),
        P(ep, None),
        P(ep, None, "tp"),
        P(ep, None, "tp"),
        P(ep, "tp", None),
    )
    return jax.shard_map(
        on_device, mesh=torus, in_specs=in_specs, out_specs=P(ep, "tp"), check_vma=False
    )
```

```python
import jax
import jax.numpy as jnp
from jax import lax
from jax.experimental import pallas as pl
from jax.experimental.pallas import tpu as pltpu
from jax.sharding import Mesh, PartitionSpec as P

PLANE = (4, 4)
CUTS = (0, 16, 24, 48)
TILE = 1024


def swap(array):
    return lax.ppermute(array, "tp", [(0, 1), (1, 0)])


def around(array, step):
    planes = lax.axis_size("z")
    pairs = []
    for plane in range(planes):
        pairs.append((2 * plane, 2 * ((plane + step) % planes)))
        pairs.append((2 * plane + 1, 2 * ((plane - step) % planes) + 1))
    return lax.ppermute(array, ("z", "tp"), pairs)


def expert_kernel(
    x, gate_a, gate_b, up_a, up_b, down_a, down_b, out,
    rows_in, into, out_of, rows_out, sums, hidden, into_sems, out_of_sems, done_sems,
):
    tiles, tile = into.shape[0], into.shape[1]
    half = gate_a.shape[1]
    units = 2 * half

    def turned(k):
        column = lax.rem(k + lax.axis_index("tp") * (tiles // 2), tiles)
        return pl.ds(pl.multiple_of(column * tile, tile), tile)

    def inward(k):
        part = pl.ds(pl.multiple_of(k * tile, tile), tile)
        rows = turned(k)
        copies = [pltpu.make_async_copy(x.at[:, part], rows_in.at[k], into_sems.at[k, 4])]
        for j, weight in enumerate((gate_a, gate_b, up_a, up_b)):
            columns = into.at[k, :, pl.ds(j * half, half)]
            copies.append(pltpu.make_async_copy(weight.at[rows, :], columns, into_sems.at[k, j]))
        return copies

    def outward(k):
        part = turned(k)
        return [
            pltpu.make_async_copy(
                weight.at[:, part], out_of.at[k, pl.ds(j * half, half), :], out_of_sems.at[k, j]
            )
            for j, weight in enumerate((down_a, down_b))
        ]

    def result(k):
        part = pl.ds(pl.multiple_of(k * tile, tile), tile)
        return pltpu.make_async_copy(rows_out.at[k], out.at[:, part], done_sems.at[k])

    for k in range(tiles):
        for copy in inward(k):
            copy.start()
    for k in range(tiles):
        for copy in outward(k):
            copy.start()
    sums[...] = jnp.zeros_like(sums)

    @pl.loop(0, tiles)
    def _(k):
        for copy in inward(k):
            copy.wait()
        sums[...] += jnp.dot(rows_in[k], into[k], preferred_element_type=jnp.float32)

    gate = sums[:, :units]
    hidden[...] = (gate / (1.0 + jnp.exp(-gate)) * sums[:, units:]).astype(jnp.bfloat16)

    @pl.loop(0, tiles)
    def _(k):
        for copy in outward(k):
            copy.wait()
        product = jnp.dot(hidden[...], out_of[k], preferred_element_type=jnp.float32)
        rows_out[k] = product.astype(jnp.bfloat16)
        result(k).start()

    for k in range(tiles):
        result(k).wait()


def run_expert(x, gates, ups, downs):
    rows, width = x.shape
    half = gates[0].shape[1]
    tile = min(TILE, width)
    tiles = width // tile
    return pl.pallas_call(
        expert_kernel,
        in_specs=[pl.BlockSpec(memory_space=pl.ANY)] * 7,
        out_specs=pl.BlockSpec(memory_space=pl.ANY),
        out_shape=jax.ShapeDtypeStruct((rows, width), jnp.bfloat16),
        scratch_shapes=[
            pltpu.VMEM((tiles, rows, tile), jnp.bfloat16),
            pltpu.VMEM((tiles, tile, 4 * half), jnp.bfloat16),
            pltpu.VMEM((tiles, 2 * half, tile), jnp.bfloat16),
            pltpu.VMEM((tiles, rows, tile), jnp.bfloat16),
            pltpu.VMEM((rows, 4 * half), jnp.float32),
            pltpu.VMEM((rows, 2 * half), jnp.bfloat16),
            pltpu.SemaphoreType.DMA((tiles, 5)),
            pltpu.SemaphoreType.DMA((tiles, 2)),
            pltpu.SemaphoreType.DMA((tiles,)),
        ],
        compiler_params=pltpu.CompilerParams(vmem_limit_bytes=60 * 1024 * 1024),
    )(x, *gates, *ups, *downs)


def tied(array, *after):
    return lax.optimization_barrier((array, *after))[0] if after else array


def exchange(array):
    return lax.all_to_all(array, ("y", "x"), split_axis=0, concat_axis=0, tiled=True)


def on_device(tokens, expert_ids, gate_levels, gate_weight, up_weight, down_weight):
    planes = lax.axis_size("z")
    plane_experts = lax.axis_size("y") * lax.axis_size("x")
    core = lax.axis_index("tp")
    tok_count, top_count = expert_ids.shape
    half_width = tokens.shape[1]
    model_width = 2 * half_width
    capacity = 3 * tok_count * top_count // (2 * planes * plane_experts)
    far = planes // 2
    half_slots = capacity // 2
    starts = [0] + [half_slots + capacity * (k - 1) for k in range(1, far + 1)]
    ends = starts[1:] + [starts[-1] + half_slots]
    chunks = list(zip(CUTS[:-1], CUTS[1:]))

    routes = jnp.concatenate([expert_ids, gate_levels], axis=1).T.astype(jnp.bfloat16)
    routes = jnp.pad(routes, ((0, tok_count - 2 * top_count), (0, 128 - tok_count)))
    blocks = [jnp.concatenate([tokens, swap(tokens), routes], axis=1)]

    first = lax.axis_index("z") * plane_experts
    plane_ids = first + jnp.arange(plane_experts, dtype=jnp.int32)
    order = jnp.arange(tok_count)
    before = (order[:, None] < order[None, :]).astype(jnp.bfloat16)

    def places(k):
        table = blocks[k][: 2 * top_count, model_width : model_width + tok_count]
        ids = table[:top_count].astype(jnp.int32)
        levels = table[top_count:].astype(jnp.float32)
        weights = levels / jnp.sum(levels, axis=0, keepdims=True)
        hits = ids[None, :, :] == plane_ids[:, None, None]
        named = jnp.any(hits, axis=1)
        scale = jnp.sum(jnp.where(hits, weights[None, :, :], 0.0), axis=1)
        rank = jnp.dot(
            named.astype(jnp.bfloat16), before, preferred_element_type=jnp.float32
        ).astype(jnp.int32)
        if k in (0, far):
            rank = rank - core * half_slots
            named = named & (rank >= 0) & (rank < half_slots)
        return jnp.where(named, rank + starts[k], -1), scale

    placed = []

    def reach(k, *after):
        while len(placed) <= k:
            if placed:
                blocks.append(around(tied(blocks[-1], *after), 1))
            placed.append(places(len(placed)))

    def within(k, chunk):
        return starts[k] < chunk[1] and chunk[0] < ends[k]

    def fits(k, chunk):
        slots = jnp.arange(chunk[0], chunk[1], dtype=jnp.int32)
        return placed[k][0][:, None, :] == slots[None, :, None]

    def pair(weight):
        return weight, swap(weight)

    gates, ups, downs = pair(gate_weight[0]), pair(up_weight[0]), pair(down_weight[0])

    def selected(index):
        chunk = chunks[index]
        rows = plane_experts * (chunk[1] - chunk[0])
        outgoing = 0.0
        for k in range(far + 1):
            if within(k, chunk):
                select = fits(k, chunk).astype(jnp.bfloat16).reshape(rows, tok_count)
                outgoing += jnp.dot(
                    select, blocks[k][:, :model_width], preferred_element_type=jnp.float32
                )
        return outgoing.astype(jnp.bfloat16).reshape(plane_experts, -1, model_width)

    def expert(arrived):
        produced = run_expert(arrived.reshape(-1, model_width), gates, ups, downs)
        return produced.reshape(plane_experts, -1, model_width)

    def last_block(index):
        return max(k for k in range(far + 1) if within(k, chunks[index]))

    reach(last_block(0))
    outgoing = [selected(0)]
    reach(2)
    reach(3, outgoing[0])
    arrived = [exchange(outgoing[0])]
    for index in range(1, len(chunks)):
        reach(last_block(index), arrived[0], *outgoing)
        outgoing.append(selected(index))
        arrived.append(exchange(outgoing[index]))
    produced = []
    for index in range(len(chunks)):
        here = tied(arrived[index], *arrived[index + 1 : len(chunks) - 1])
        produced.append(expert(here))

    returns = [None] * len(chunks)
    before_it = (*produced[:-1], arrived[-1])
    for index in (1, 2, 0):
        returns[index] = exchange(tied(produced[index], *before_it))
        before_it = (returns[index],)
    returns = [one.reshape(-1, model_width) for one in returns]

    totals = [0.0, 0.0]
    for k in reversed(range(far + 1)):
        for index in reversed(range(len(chunks))):
            chunk = chunks[index]
            if within(k, chunk):
                mix = jnp.where(fits(k, chunk), placed[k][1][:, None, :], 0.0)
                mix = mix.astype(jnp.bfloat16).reshape(-1, tok_count)
                for half in range(2):
                    totals[half] += lax.dot_general(
                        mix,
                        returns[index][:, half * half_width : (half + 1) * half_width],
                        (((0,), (0,)), ((), ())),
                        preferred_element_type=jnp.float32,
                    )
        if k > 0:
            kept, given = [total.astype(jnp.bfloat16) for total in totals]
            kept = tied(kept, given)
            given = around(given, -1).astype(jnp.float32)
            kept = around(kept, -1).astype(jnp.float32)
            totals = [kept, given]
    kept, given = totals
    given = swap(given.astype(jnp.bfloat16)).astype(jnp.float32)
    return (kept + given).astype(jnp.bfloat16)


def solution(mesh):
    n_ep, n_tp = mesh.shape["ep"], mesh.shape["tp"]
    n_y, n_x = PLANE
    torus = Mesh(
        mesh.devices.reshape(n_ep // (n_y * n_x), n_y, n_x, n_tp), ("z", "y", "x", "tp")
    )
    ep = ("z", "y", "x")
    in_specs = (
        P(ep, "tp"),
        P(ep, None),
        P(ep, None),
        P(ep, None, "tp"),
        P(ep, None, "tp"),
        P(ep, "tp", None),
    )
    return jax.shard_map(
        on_device, mesh=torus, in_specs=in_specs, out_specs=P(ep, "tp"), check_vma=False
    )
```
